32 devices in a mesh: row: 8 (over z, x), col: 4 (over y, core).
Axes of the slice: x: 2, y: 2, z: 4, core: 2. Of those that a mesh axis runs over, the one named last changes fastest.
Arguments:
- psi: bfloat16 [8, 8, 3, 256, 256], P('row', None, None, 'col'), may hold values from -6 to 6
- left_ops: bfloat16 [8, 8, 32, 256, 256], P('row', None, 'col'), may hold values from -0.375 to 0.375
- right_ops: bfloat16 [8, 8, 32, 256, 256], P('row', None, 'col'), may hold values from -0.0625 to 0.0625
- mpo_pattern: int32 [8, 8, 32], P('row', None, 'col'), may hold values 0 or 1
- block_sizes: int32 [2, 8, 8], P(None, 'row'), may hold values from 1 to 256, 1280 in all within a row
Outputs:
- h_psi: bfloat16 [8, 8, 3, 256, 256], P('row', None, None, 'col')
The draws below stay inside these ranges and needn't reach their ends.
Inputs may be any that keep to these rules, and one draw needn't show every extreme that they name: `block_sizes`: for each index and sector a, the 8 sizes along the last dimension sum to 1280.
All inputs are finite; a program needn't handle non-finite values. No bound on the sum of `mpo_pattern` on one device may be relied on, other than what follows from the above.
Results may differ from the reference program's by a relative error of at most 0.005.
Values may be sent and summed in bfloat16 or wider, within the bound.
A program may use at most 128 MiB of HBM per device.

```python
import math
import jax
import jax.numpy as jnp
import numpy as np
from jax import lax

BLK = 256
W = 32
NVEC = 3
NA = 8
NB = 8


def place_ends(result, rng, smallest, high):
    longest = result.shape.index(max(result.shape))
    spots = []
    for shift in (0, 1):
        where = [jax.random.randint(jax.random.fold_in(rng, axis), (), 0, length) for axis, length in enumerate(result.shape)]
        where[longest] = (where[longest] + shift) % result.shape[longest]
        spots.append(tuple(where))
    return result.at[spots[0]].set(smallest).at[spots[1]].set(high)


def level_of(key, extent, cuts, low, high):
    loudness = 1.0
    for axis_at, blocks in cuts:
        steps = jax.random.uniform(jax.random.fold_in(jax.random.fold_in(key, 6), axis_at), (blocks,), jnp.float32, low / len(cuts), high / len(cuts))
        loudness = loudness * jnp.repeat(jnp.exp(steps), extent[axis_at] // blocks).reshape((-1,) + (1,) * (len(extent) - 1 - axis_at))
    return loudness


def profile(number_of, total, most, skew):
    portions = [(1 << 20) // math.isqrt(grade ** skew) + 1 for grade in range(2, number_of + 1)]
    spare, holding = total - most - (number_of - 1), [1] * (number_of - 1)
    while spare > 0:
        candidates = [i for i in range(number_of - 1) if holding[i] < most]
        pool, budget = sum([portions[i] for i in candidates]), spare
        for i in candidates:
            addition = min(most - holding[i], max(1, budget * portions[i] // pool), spare)
            holding[i] = holding[i] + addition
            spare = spare - addition
    return np.array([most] + holding)


def ragged_sizes(stream_key, number_of, total, limit, slope):
    if number_of == 2:
        one = jax.random.randint(stream_key, (), max(1, total - limit), min(limit, total - 1) + 1)
        return jnp.stack([one, total - one])
    tallies = jnp.asarray(profile(number_of, total, limit, slope), jnp.int32)
    couples = (number_of - 1) // 2
    source_of, sink = tallies[1:1 + 2 * couples:2], tallies[2:2 + 2 * couples:2]
    room = jnp.minimum(source_of - 1, limit - sink)
    shifted = jax.random.randint(jax.random.fold_in(stream_key, 1), (couples,), 0, 1 << 20) % (room + 1)
    tallies = tallies.at[1:1 + 2 * couples:2].set(source_of - shifted).at[2:2 + 2 * couples:2].set(sink + shifted)
    return tallies[jax.random.permutation(jax.random.fold_in(stream_key, 2), number_of)]


def centred(rng, extent, deviation, reach, pieces=(), held_as=jnp.bfloat16):
    array = jax.random.normal(rng, extent, jnp.float32) * deviation
    if len(pieces) > 0:
        array = level_of(rng, extent, pieces, -0.22, 0.18) * array
    return jnp.clip(array, min=-reach, max=reach).astype(held_as)


def setup_inputs(seed: int = 0) -> dict:
    key_of = jax.random.split(jax.random.key(seed), 6)
    return {
        "psi": centred(key_of[0], (NA, NB, NVEC, BLK, BLK), 1.0, 6.0, ((0, 8), (3, 4))),
        "left_ops": centred(key_of[1], (NA, NB, W, BLK, BLK), BLK ** -0.5, 0.375, ((0, 8), (2, 4))),
        "right_ops": centred(key_of[2], (NB, NA, W, BLK, BLK), (BLK * W) ** -0.5, 0.0625, ((0, 8), (2, 4))),
        "mpo_pattern": place_ends((jax.random.randint(key_of[3], (NA, NB, W), 0, 4) < 3).astype(jnp.int32), jax.random.fold_in(key_of[3], 1), 0, 1),
        "block_sizes": jax.vmap(lambda own: ragged_sizes(own, NB, NB * BLK * 5 // 8, BLK, 2))(jax.random.split(key_of[4], 2 * NA)).reshape((2, NA, NB)).astype(jnp.int32),
    }


def reference(psi, left_ops, right_ops, mpo_pattern, block_sizes):
    index = jnp.arange(BLK, dtype=jnp.int32)

    def one_sector(sector):
        live_rows = index[None, :] < block_sizes[0, sector][:, None]
        live_cols = index[None, :] < block_sizes[1, sector][:, None]
        keep = live_rows[:, None, :, None] & live_cols[:, None, None, :]
        live = jnp.where(keep, psi[sector], jnp.zeros((), jnp.bfloat16)).astype(jnp.bfloat16)
        terms = jnp.einsum("bkrm,bvmc->bkvrc", left_ops[sector].astype(jnp.float32), live.astype(jnp.float32))
        terms = (terms * mpo_pattern[sector][:, :, None, None, None].astype(jnp.float32)).astype(jnp.bfloat16)
        right = right_ops[:, sector]
        total = jnp.einsum("bkvrm,bkcm->bvrc", terms.astype(jnp.float32), right.astype(jnp.float32))
        return jnp.where(keep, total, jnp.zeros((), jnp.float32)).astype(jnp.bfloat16)

    return lax.map(one_sector, jnp.arange(NA, dtype=jnp.int32))
```

```python
import functools

import jax
import jax.numpy as jnp
from jax import lax
from jax.experimental import pallas as pl
from jax.experimental.pallas import tpu as pltpu
from jax.sharding import PartitionSpec as P

MESH = pl.DeviceIdType.MESH
PARTS = 2


def partner(me, step, n):
    if n & (n - 1):
        return lax.rem(me + step, n)
    total, bit = 0, 1
    while bit < n:
        total = total + bit * (((me // bit) % 2 + (step // bit) % 2) % 2)
        bit *= 2
    return total


def source(me, step, n):
    if n & (n - 1):
        return lax.rem(me + n - step, n)
    return partner(me, step, n)


def kernel(
    n, nc, psi, left, right, pattern, sizes, out,
    whole, landed, lefts, live, terms, part, sums, own,
    psi_send, psi_recv, psi_own, right_send, right_recv, right_own, left_sem, sum_send, sum_recv,
):
    row, col = lax.axis_index("row"), lax.axis_index("col")
    channels, blk = left.shape[2], left.shape[3]
    vectors, height = psi.shape[2], psi.shape[3]
    width = blk // PARTS
    ahead = n // 2 + 1

    barrier = pltpu.get_barrier_semaphore()
    for step in range(1, n):
        pl.semaphore_signal(
            barrier, inc=1, device_id={"row": lax.rem(row + step, n)}, device_id_type=MESH
        )
    for step in range(1, nc):
        pl.semaphore_signal(
            barrier, inc=1, device_id={"col": lax.rem(col + step, nc)}, device_id_type=MESH
        )
    pl.semaphore_wait(barrier, n + nc - 2)

    def right_copy(step, p):
        to = partner(row, step, n)
        return pltpu.make_async_remote_copy(
            src_ref=right.at[0, to, :, pl.ds(p * width, width), :],
            dst_ref=landed.at[row, p],
            send_sem=right_send.at[step, p],
            recv_sem=right_recv.at[row, p],
            device_id={"row": to},
            device_id_type=MESH,
        )

    def right_arrival(step, p):
        b = source(row, step, n)
        return pltpu.make_async_remote_copy(
            src_ref=landed.at[b, p],
            dst_ref=landed.at[b, p],
            send_sem=right_send.at[step, p],
            recv_sem=right_recv.at[b, p],
            device_id={"row": b},
            device_id_type=MESH,
        )

    def right_local(p):
        return pltpu.make_async_copy(
            right.at[0, row, :, pl.ds(p * width, width), :], landed.at[row, p], right_own.at[p]
        )

    def psi_copy(off):
        return pltpu.make_async_remote_copy(
            src_ref=psi.at[0],
            dst_ref=whole.at[col],
            send_sem=psi_send.at[off],
            recv_sem=psi_recv.at[col],
            device_id={"col": lax.rem(col + off, nc)},
            device_id_type=MESH,
        )

    def psi_arrival(off):
        c = lax.rem(col + nc - off, nc)
        return pltpu.make_async_remote_copy(
            src_ref=psi.at[0],
            dst_ref=whole.at[c],
            send_sem=psi_send.at[off],
            recv_sem=psi_recv.at[c],
            device_id={"col": c},
            device_id_type=MESH,
        )

    def left_copy(step):
        return pltpu.make_async_copy(
            left.at[0, source(row, step, n)], lefts.at[step % 2], left_sem.at[step % 2]
        )

    def sum_copy(step, p, off):
        to = lax.rem(col + off, nc)
        b = source(row, step, n)
        return pltpu.make_async_remote_copy(
            src_ref=part.at[step % 2, p, to],
            dst_ref=sums.at[off - 1, b, p],
            send_sem=sum_send.at[off - 1, step % 2, p],
            recv_sem=sum_recv.at[off - 1, b, p],
            device_id={"col": to},
            device_id_type=MESH,
        )

    psi_local = pltpu.make_async_copy(psi.at[0], whole.at[col], psi_own)
    psi_local.start()
    left_copy(0).start()
    for p in range(PARTS):
        right_local(p).start()
    for off in range(1, nc):
        psi_copy(off).start()

    @pl.loop(1, min(ahead, n - 1) + 1)
    def _(step):
        for p in range(PARTS):
            right_copy(step, p).start()

    psi_local.wait()
    for off in range(1, nc):
        psi_arrival(off).wait_recv()

    def finish(step):
        b = source(row, step, n)
        live_rows, live_cols = sizes[0, 0, b], sizes[1, 0, b]
        r = lax.broadcasted_iota(jnp.int32, (height, width), 0) + col * height
        c = lax.broadcasted_iota(jnp.int32, (height, width), 1)
        for p in range(PARTS):
            for off in range(1, nc):
                sum_copy(step, p, off).wait_recv()
            keep = (r < live_rows) & (c + p * width < live_cols)
            for v in range(vectors):
                total = own[b, p, v]
                for off in range(1, nc):
                    total = total + sums[off - 1, b, p, v]
                out[0, b, v, :, p * width : (p + 1) * width] = jnp.where(keep, total, 0.0).astype(
                    out.dtype
                )

    @pl.loop(0, n)
    def _(step):
        b = source(row, step, n)

        @pl.when(step + 1 < n)
        def _():
            left_copy(step + 1).start()

        live_rows, live_cols = sizes[0, 0, b], sizes[1, 0, b]
        r = lax.broadcasted_iota(jnp.int32, (height, blk), 0)
        c = lax.broadcasted_iota(jnp.int32, (height, blk), 1)
        for g in range(nc):
            keep = (r + g * height < live_rows) & (c < live_cols)
            for v in range(vectors):
                block = whole[g, b, v].astype(jnp.float32)
                live[g * height : (g + 1) * height, v * blk : (v + 1) * blk] = jnp.where(
                    keep, block, 0.0
                ).astype(live.dtype)

        left_copy(step).wait()

        @pl.loop(0, channels)
        def _(k):
            acts = pattern[0, b, k].astype(jnp.float32)
            for v in range(vectors):
                term = jnp.dot(
                    lefts[step % 2, k],
                    live[:, v * blk : (v + 1) * blk],
                    preferred_element_type=jnp.float32,
                )
                terms[v, k] = (term * acts).astype(terms.dtype)

        for p in range(PARTS):

            @pl.when(step == 0)
            def _():
                right_local(p).wait()

            @pl.when(step > 0)
            def _():
                right_arrival(step, p).wait_recv()

            @pl.when(step >= 2)
            def _():
                for off in range(1, nc):
                    sum_copy(step - 2, p, off).wait_send()

            @pl.loop(0, vectors)
            def _(v):
                total = jnp.zeros((blk, width), jnp.float32)
                for k in range(channels):
                    total = total + lax.dot_general(
                        terms[v, k],
                        landed[b, p, k],
                        (((1,), (1,)), ((), ())),
                        preferred_element_type=jnp.float32,
                    )
                for g in range(nc):
                    part[step % 2, p, g, v] = total[g * height : (g + 1) * height]

            own[b, p] = part[step % 2, p, col]
            for off in range(1, nc):
                sum_copy(step, p, off).start()

        @pl.when((step >= ahead - 1) & (step + 2 < n))
        def _():
            for p in range(PARTS):
                right_copy(step + 2, p).start()

        @pl.when(step >= 1)
        def _():
            finish(step - 1)

    finish(n - 1)

    @pl.loop(1, n)
    def _(step):
        for p in range(PARTS):
            right_copy(step, p).wait_send()

    for off in range(1, nc):
        psi_copy(off).wait_send()
    for step in range(max(0, n - 2), n):
        for p in range(PARTS):
            for off in range(1, nc):
                sum_copy(step, p, off).wait_send()


def solution(mesh):
    n, nc = mesh.shape["row"], mesh.shape["col"]

    def shards(psi, left_ops, right_ops, mpo_pattern, block_sizes):
        _, nb, vectors, height, blk = psi.shape
        channels = left_ops.shape[2]
        width = blk // PARTS
        dma = pltpu.SemaphoreType.DMA
        flops = 4 * nb * channels * vectors * blk**3
        return pl.pallas_call(
            functools.partial(kernel, n, nc),
            out_shape=jax.ShapeDtypeStruct(psi.shape, jnp.bfloat16),
            in_specs=[pl.BlockSpec(memory_space=pl.ANY)] * 3
            + [pl.BlockSpec(memory_space=pltpu.SMEM)] * 2,
            out_specs=pl.BlockSpec(memory_space=pltpu.VMEM),
            scratch_shapes=[
                pltpu.VMEM((nc, nb, vectors, height, blk), jnp.bfloat16),
                pltpu.VMEM((nb, PARTS, channels, width, blk), jnp.bfloat16),
                pltpu.VMEM((2, channels, blk, blk), jnp.bfloat16),
                pltpu.VMEM((blk, vectors * blk), jnp.bfloat16),
                pltpu.VMEM((vectors, channels, blk, blk), jnp.bfloat16),
                pltpu.VMEM((2, PARTS, nc, vectors, height, width), jnp.float32),
                pltpu.VMEM((nc - 1, nb, PARTS, vectors, height, width), jnp.float32),
                pltpu.VMEM((nb, PARTS, vectors, height, width), jnp.float32),
                dma((nc,)),
                dma((nc,)),
                dma,
                dma((n, PARTS)),
                dma((n, PARTS)),
                dma((PARTS,)),
                dma((2,)),
                dma((nc - 1, 2, PARTS)),
                dma((nc - 1, nb, PARTS)),
            ],
            compiler_params=pltpu.CompilerParams(
                collective_id=0, has_side_effects=True, vmem_limit_bytes=56 * 2**20
            ),
            cost_estimate=pl.CostEstimate(
                flops=flops, bytes_accessed=4 * left_ops.size, transcendentals=0
            ),
        )(psi, left_ops, right_ops, mpo_pattern, block_sizes)

    in_specs = (
        P("row", None, None, "col", None),
        P("row", None, "col", None, None),
        P("row", None, "col", None, None),
        P("row", None, "col"),
        P(None, "row", None),
    )
    out_specs = P("row", None, None, "col", None)
    return jax.shard_map(shards, mesh=mesh, in_specs=in_specs, out_specs=out_specs, check_vma=False)
```

```python
import functools

import jax
import jax.numpy as jnp
from jax import lax
from jax.experimental import pallas as pl
from jax.experimental.pallas import tpu as pltpu
from jax.sharding import PartitionSpec as P

MESH = pl.DeviceIdType.MESH
PARTS = 2
FLIGHT = 3


def partner(me, step, n):
    if n & (n - 1):
        return lax.rem(me + step, n)
    total, bit = 0, 1
    while bit < n:
        total = total + bit * (((me // bit) % 2 + (step // bit) % 2) % 2)
        bit *= 2
    return total


def source(me, step, n):
    if n & (n - 1):
        return lax.rem(me + n - step, n)
    return partner(me, step, n)


def kernel(
    n, nc, psi, left, right, pattern, sizes, out,
    whole, landed, lefts, live, terms, part, sums, own,
    psi_send, psi_recv, psi_own, right_send, right_recv, right_own, left_sem, sum_send, sum_recv,
):
    row, col = lax.axis_index("row"), lax.axis_index("col")
    channels, blk = left.shape[2], left.shape[3]
    vectors, height = psi.shape[2], psi.shape[3]
    width = blk // PARTS
    far = n // 2

    barrier = pltpu.get_barrier_semaphore()
    for step in range(1, n):
        pl.semaphore_signal(
            barrier, inc=1, device_id={"row": lax.rem(row + step, n)}, device_id_type=MESH
        )
    for step in range(1, nc):
        pl.semaphore_signal(
            barrier, inc=1, device_id={"col": lax.rem(col + step, nc)}, device_id_type=MESH
        )

    def right_copy(step, p):
        to = partner(row, step, n)
        return pltpu.make_async_remote_copy(
            src_ref=right.at[0, to, :, pl.ds(p * width, width), :],
            dst_ref=landed.at[row, p],
            send_sem=right_send.at[step, p],
            recv_sem=right_recv.at[row, p],
            device_id={"row": to},
            device_id_type=MESH,
        )

    def right_arrival(step, p):
        b = source(row, step, n)
        return pltpu.make_async_remote_copy(
            src_ref=landed.at[b, p],
            dst_ref=landed.at[b, p],
            send_sem=right_send.at[step, p],
            recv_sem=right_recv.at[b, p],
            device_id={"row": b},
            device_id_type=MESH,
        )

    def right_local(p):
        return pltpu.make_async_copy(
            right.at[0, row, :, pl.ds(p * width, width), :], landed.at[row, p], right_own.at[p]
        )

    def psi_copy(off):
        return pltpu.make_async_remote_copy(
            src_ref=psi.at[0],
            dst_ref=whole.at[col],
            send_sem=psi_send.at[off],
            recv_sem=psi_recv.at[col],
            device_id={"col": lax.rem(col + off, nc)},
            device_id_type=MESH,
        )

    def psi_arrival(off):
        c = lax.rem(col + nc - off, nc)
        return pltpu.make_async_remote_copy(
            src_ref=psi.at[0],
            dst_ref=whole.at[c],
            send_sem=psi_send.at[off],
            recv_sem=psi_recv.at[c],
            device_id={"col": c},
            device_id_type=MESH,
        )

    def left_copy(step):
        return pltpu.make_async_copy(
            left.at[0, source(row, step, n)], lefts.at[step % 2], left_sem.at[step % 2]
        )

    def sum_copy(step, p, v, off):
        to = lax.rem(col + off, nc)
        b = source(row, step, n)
        return pltpu.make_async_remote_copy(
            src_ref=part.at[step % 2, p, to, v],
            dst_ref=sums.at[off - 1, b, p, v],
            send_sem=sum_send.at[off - 1, step % 2, p, v],
            recv_sem=sum_recv.at[off - 1, b, p, v],
            device_id={"col": to},
            device_id_type=MESH,
        )

    psi_local = pltpu.make_async_copy(psi.at[0], whole.at[col], psi_own)
    psi_local.start()
    left_copy(0).start()
    for p in range(PARTS):
        right_local(p).start()
    pl.semaphore_wait(barrier, n + nc - 2)
    for off in range(1, nc):
        psi_copy(off).start()

    far_span, near_span = (far, min(far + FLIGHT, n)), (1, far)
    for span in (near_span, far_span):

        @pl.loop(*span)
        def _(step):
            for p in range(PARTS):
                right_copy(step, p).start()

    psi_local.wait()
    for off in range(1, nc):
        psi_arrival(off).wait_recv()

    def finish(step):
        b = source(row, step, n)
        live_rows, live_cols = sizes[0, 0, b], sizes[1, 0, b]
        r = lax.broadcasted_iota(jnp.int32, (height, width), 0) + col * height
        c = lax.broadcasted_iota(jnp.int32, (height, width), 1)
        for p in range(PARTS):
            keep = (r < live_rows) & (c + p * width < live_cols)
            for v in range(vectors):
                for off in range(1, nc):
                    sum_copy(step, p, v, off).wait_recv()
                total = own[b, p, v]
                for off in range(1, nc):
                    total = total + sums[off - 1, b, p, v]
                out[0, b, v, :, p * width : (p + 1) * width] = jnp.where(keep, total, 0.0).astype(
                    out.dtype
                )

    @pl.loop(0, n)
    def _(step):
        b = source(row, step, n)

        @pl.when(step + 1 < n)
        def _():
            left_copy(step + 1).start()

        live_rows, live_cols = sizes[0, 0, b], sizes[1, 0, b]
        r = lax.broadcasted_iota(jnp.int32, (height, blk), 0)
        c = lax.broadcasted_iota(jnp.int32, (height, blk), 1)
        for g in range(nc):
            keep = (r + g * height < live_rows) & (c < live_cols)
            for v in range(vectors):
                block = whole[g, b, v].astype(jnp.float32)
                live[g * height : (g + 1) * height, v * blk : (v + 1) * blk] = jnp.where(
                    keep, block, 0.0
                ).astype(live.dtype)

        left_copy(step).wait()

        @pl.loop(0, channels)
        def _(k):
            acts = pattern[0, b, k].astype(jnp.float32)
            for v in range(vectors):
                term = jnp.dot(
                    lefts[step % 2, k],
                    live[:, v * blk : (v + 1) * blk],
                    preferred_element_type=jnp.float32,
                )
                terms[v, k] = (term * acts).astype(terms.dtype)

        for p in range(PARTS):

            @pl.when(step == 0)
            def _():
                right_local(p).wait()

            @pl.when(step > 0)
            def _():
                right_arrival(step, p).wait_recv()

            @pl.when((step >= far) & (step + FLIGHT < n))
            def _():
                right_copy(step + FLIGHT, p).start()

            @pl.when(step >= 2)
            def _():
                for v in range(vectors):
                    for off in range(1, nc):
                        sum_copy(step - 2, p, v, off).wait_send()

            @pl.loop(0, vectors)
            def _(v):
                total = jnp.zeros((blk, width), jnp.float32)
                for k in range(channels):
                    total = total + lax.dot_general(
                        terms[v, k],
                        landed[b, p, k],
                        (((1,), (1,)), ((), ())),
                        preferred_element_type=jnp.float32,
                    )
                for g in range(nc):
                    part[step % 2, p, g, v] = total[g * height : (g + 1) * height]
                for off in range(1, nc):
                    sum_copy(step, p, v, off).start()
                own[b, p, v] = part[step % 2, p, col, v]

        @pl.when(step >= 1)
        def _():
            finish(step - 1)

    finish(n - 1)

    @pl.loop(1, n)
    def _(step):
        for p in range(PARTS):
            right_copy(step, p).wait_send()

    for off in range(1, nc):
        psi_copy(off).wait_send()
    for step in range(max(0, n - 2), n):
        for p in range(PARTS):
            for v in range(vectors):
                for off in range(1, nc):
                    sum_copy(step, p, v, off).wait_send()


def solution(mesh):
    n, nc = mesh.shape["row"], mesh.shape["col"]

    def shards(psi, left_ops, right_ops, mpo_pattern, block_sizes):
        _, nb, vectors, height, blk = psi.shape
        channels = left_ops.shape[2]
        width = blk // PARTS
        dma = pltpu.SemaphoreType.DMA
        flops = 4 * nb * channels * vectors * blk**3
        return pl.pallas_call(
            functools.partial(kernel, n, nc),
            out_shape=jax.ShapeDtypeStruct(psi.shape, jnp.bfloat16),
            in_specs=[pl.BlockSpec(memory_space=pl.ANY)] * 3
            + [pl.BlockSpec(memory_space=pltpu.SMEM)] * 2,
            out_specs=pl.BlockSpec(memory_space=pltpu.VMEM),
            scratch_shapes=[
                pltpu.VMEM((nc, nb, vectors, height, blk), jnp.bfloat16),
                pltpu.VMEM((nb, PARTS, channels, width, blk), jnp.bfloat16),
                pltpu.VMEM((2, channels, blk, blk), jnp.bfloat16),
                pltpu.VMEM((blk, vectors * blk), jnp.bfloat16),
                pltpu.VMEM((vectors, channels, blk, blk), jnp.bfloat16),
                pltpu.VMEM((2, PARTS, nc, vectors, height, width), jnp.float32),
                pltpu.VMEM((nc - 1, nb, PARTS, vectors, height, width), jnp.float32),
                pltpu.VMEM((nb, PARTS, vectors, height, width), jnp.float32),
                dma((nc,)),
                dma((nc,)),
                dma,
                dma((n, PARTS)),
                dma((n, PARTS)),
                dma((PARTS,)),
                dma((2,)),
                dma((nc - 1, 2, PARTS, vectors)),
                dma((nc - 1, nb, PARTS, vectors)),
            ],
            compiler_params=pltpu.CompilerParams(
                collective_id=0, has_side_effects=True, vmem_limit_bytes=56 * 2**20
            ),
            cost_estimate=pl.CostEstimate(
                flops=flops, bytes_accessed=4 * left_ops.size, transcendentals=0
            ),
        )(psi, left_ops, right_ops, mpo_pattern, block_sizes)

    in_specs = (
        P("row", None, None, "col", None),
        P("row", None, "col", None, None),
        P("row", None, "col", None, None),
        P("row", None, "col"),
        P(None, "row", None),
    )
    out_specs = P("row", None, None, "col", None)
    return jax.shard_map(shards, mesh=mesh, in_specs=in_specs, out_specs=out_specs, check_vma=False)
```

```python
import functools

import jax
import jax.numpy as jnp
from jax import lax
from jax.experimental import pallas as pl
from jax.experimental.pallas import tpu as pltpu
from jax.sharding import PartitionSpec as P

MESH = pl.DeviceIdType.MESH
PARTS = 2
FLIGHT = 3


def partner(me, step, n):
    if n & (n - 1):
        return lax.rem(me + step, n)
    total, bit = 0, 1
    while bit < n:
        total = total + bit * (((me // bit) % 2 + (step // bit) % 2) % 2)
        bit *= 2
    return total


def source(me, step, n):
    if n & (n - 1):
        return lax.rem(me + n - step, n)
    return partner(me, step, n)


def kernel(
    n, nc, psi, left, right, pattern, sizes, out,
    whole, landed, lefts, live, terms, part, sums, own,
    psi_send, psi_recv, psi_own, right_send, right_recv, right_own, left_sem, sum_send, sum_recv,
):
    row, col = lax.axis_index("row"), lax.axis_index("col")
    channels, blk = left.shape[2], left.shape[3]
    vectors, height = psi.shape[2], psi.shape[3]
    width = blk // PARTS
    far = n // 2

    barrier = pltpu.get_barrier_semaphore()
    for step in range(1, n):
        pl.semaphore_signal(
            barrier, inc=1, device_id={"row": lax.rem(row + step, n)}, device_id_type=MESH
        )
    for step in range(1, nc):
        pl.semaphore_signal(
            barrier, inc=1, device_id={"col": lax.rem(col + step, nc)}, device_id_type=MESH
        )

    def right_copy(step, p):
        to = partner(row, step, n)
        return pltpu.make_async_remote_copy(
            src_ref=right.at[0, to, :, pl.ds(p * width, width), :],
            dst_ref=landed.at[row, p],
            send_sem=right_send.at[step, p],
            recv_sem=right_recv.at[row, p],
            device_id={"row": to},
            device_id_type=MESH,
        )

    def right_arrival(step, p):
        b = source(row, step, n)
        return pltpu.make_async_remote_copy(
            src_ref=landed.at[b, p],
            dst_ref=landed.at[b, p],
            send_sem=right_send.at[step, p],
            recv_sem=right_recv.at[b, p],
            device_id={"row": b},
            device_id_type=MESH,
        )

    def right_local(p):
        return pltpu.make_async_copy(
            right.at[0, row, :, pl.ds(p * width, width), :], landed.at[row, p], right_own.at[p]
        )

    def psi_copy(off):
        return pltpu.make_async_remote_copy(
            src_ref=psi.at[0],
            dst_ref=whole.at[col],
            send_sem=psi_send.at[off],
            recv_sem=psi_recv.at[col],
            device_id={"col": lax.rem(col + off, nc)},
            device_id_type=MESH,
        )

    def psi_arrival(off):
        c = lax.rem(col + nc - off, nc)
        return pltpu.make_async_remote_copy(
            src_ref=psi.at[0],
            dst_ref=whole.at[c],
            send_sem=psi_send.at[off],
            recv_sem=psi_recv.at[c],
            device_id={"col": c},
            device_id_type=MESH,
        )

    def left_copy(step):
        return pltpu.make_async_copy(
            left.at[0, source(row, step, n)], lefts.at[step % 2], left_sem.at[step % 2]
        )

    def sum_copy(step, p, v, off):
        to = lax.rem(col + off, nc)
        b = source(row, step, n)
        return pltpu.make_async_remote_copy(
            src_ref=part.at[step % 2, p, to, v],
            dst_ref=sums.at[off - 1, b, p, v],
            send_sem=sum_send.at[off - 1, step % 2, p, v],
            recv_sem=sum_recv.at[off - 1, b, p, v],
            device_id={"col": to},
            device_id_type=MESH,
        )

    psi_local = pltpu.make_async_copy(psi.at[0], whole.at[col], psi_own)
    psi_local.start()
    left_copy(0).start()
    for p in range(PARTS):
        right_local(p).start()
    pl.semaphore_wait(barrier, n + nc - 2)

    far_span, near_span = (far, min(far + FLIGHT, n)), (1, far)
    for span in (far_span, near_span):

        @pl.loop(*span)
        def _(step):
            for p in range(PARTS):
                right_copy(step, p).start()

    for off in range(1, nc):
        psi_copy(off).start()
    psi_local.wait()
    for off in range(1, nc):
        psi_arrival(off).wait_recv()

    def finish(step):
        b = source(row, step, n)
        live_rows, live_cols = sizes[0, 0, b], sizes[1, 0, b]
        r = lax.broadcasted_iota(jnp.int32, (height, width), 0) + col * height
        c = lax.broadcasted_iota(jnp.int32, (height, width), 1)
        for p in range(PARTS):
            keep = (r < live_rows) & (c + p * width < live_cols)
            for v in range(vectors):
                for off in range(1, nc):
                    sum_copy(step, p, v, off).wait_recv()
                total = own[b, p, v]
                for off in range(1, nc):
                    total = total + sums[off - 1, b, p, v]
                out[0, b, v, :, p * width : (p + 1) * width] = jnp.where(keep, total, 0.0).astype(
                    out.dtype
                )

    @pl.loop(0, n)
    def _(step):
        b = source(row, step, n)

        @pl.when(step + 1 < n)
        def _():
            left_copy(step + 1).start()

        live_rows, live_cols = sizes[0, 0, b], sizes[1, 0, b]
        r = lax.broadcasted_iota(jnp.int32, (height, blk), 0)
        c = lax.broadcasted_iota(jnp.int32, (height, blk), 1)
        for g in range(nc):
            keep = (r + g * height < live_rows) & (c < live_cols)
            for v in range(vectors):
                block = whole[g, b, v].astype(jnp.float32)
                live[g * height : (g + 1) * height, v * blk : (v + 1) * blk] = jnp.where(
                    keep, block, 0.0
                ).astype(live.dtype)

        left_copy(step).wait()

        @pl.loop(0, channels)
        def _(k):
            acts = pattern[0, b, k].astype(jnp.float32)
            for v in range(vectors):
                term = jnp.dot(
                    lefts[step % 2, k],
                    live[:, v * blk : (v + 1) * blk],
                    preferred_element_type=jnp.float32,
                )
                terms[v, k] = (term * acts).astype(terms.dtype)

        for p in range(PARTS):

            @pl.when(step == 0)
            def _():
                right_local(p).wait()

            @pl.when(step > 0)
            def _():
                right_arrival(step, p).wait_recv()

            @pl.when((step >= far) & (step + FLIGHT < n))
            def _():
                right_copy(step + FLIGHT, p).start()

            @pl.when(step >= 2)
            def _():
                for v in range(vectors):
                    for off in range(1, nc):
                        sum_copy(step - 2, p, v, off).wait_send()

            @pl.loop(0, vectors)
            def _(v):
                total = jnp.zeros((blk, width), jnp.float32)
                for k in range(channels):
                    total = total + lax.dot_general(
                        terms[v, k],
                        landed[b, p, k],
                        (((1,), (1,)), ((), ())),
                        preferred_element_type=jnp.float32,
                    )
                for g in range(nc):
                    part[step % 2, p, g, v] = total[g * height : (g + 1) * height]
                for off in range(1, nc):
                    sum_copy(step, p, v, off).start()
                own[b, p, v] = part[step % 2, p, col, v]

        @pl.when(step >= 1)
        def _():
            finish(step - 1)

    finish(n - 1)

    @pl.loop(1, n)
    def _(step):
        for p in range(PARTS):
            right_copy(step, p).wait_send()

    for off in range(1, nc):
        psi_copy(off).wait_send()
    for step in range(max(0, n - 2), n):
        for p in range(PARTS):
            for v in range(vectors):
                for off in range(1, nc):
                    sum_copy(step, p, v, off).wait_send()


def solution(mesh):
    n, nc = mesh.shape["row"], mesh.shape["col"]

    def shards(psi, left_ops, right_ops, mpo_pattern, block_sizes):
        _, nb, vectors, height, blk = psi.shape
        channels = left_ops.shape[2]
        width = blk // PARTS
        dma = pltpu.SemaphoreType.DMA
        flops = 4 * nb * channels * vectors * blk**3
        return pl.pallas_call(
            functools.partial(kernel, n, nc),
            out_shape=jax.ShapeDtypeStruct(psi.shape, jnp.bfloat16),
            in_specs=[pl.BlockSpec(memory_space=pl.ANY)] * 3
            + [pl.BlockSpec(memory_space=pltpu.SMEM)] * 2,
            out_specs=pl.BlockSpec(memory_space=pltpu.VMEM),
            scratch_shapes=[
                pltpu.VMEM((nc, nb, vectors, height, blk), jnp.bfloat16),
                pltpu.VMEM((nb, PARTS, channels, width, blk), jnp.bfloat16),
                pltpu.VMEM((2, channels, blk, blk), jnp.bfloat16),
                pltpu.VMEM((blk, vectors * blk), jnp.bfloat16),
                pltpu.VMEM((vectors, channels, blk, blk), jnp.bfloat16),
                pltpu.VMEM((2, PARTS, nc, vectors, height, width), jnp.float32),
                pltpu.VMEM((nc - 1, nb, PARTS, vectors, height, width), jnp.float32),
                pltpu.VMEM((nb, PARTS, vectors, height, width), jnp.float32),
                dma((nc,)),
                dma((nc,)),
                dma,
                dma((n, PARTS)),
                dma((n, PARTS)),
                dma((PARTS,)),
                dma((2,)),
                dma((nc - 1, 2, PARTS, vectors)),
                dma((nc - 1, nb, PARTS, vectors)),
            ],
            compiler_params=pltpu.CompilerParams(
                collective_id=0, has_side_effects=True, vmem_limit_bytes=56 * 2**20
            ),
            cost_estimate=pl.CostEstimate(
                flops=flops, bytes_accessed=4 * left_ops.size, transcendentals=0
            ),
        )(psi, left_ops, right_ops, mpo_pattern, block_sizes)

    in_specs = (
        P("row", None, None, "col", None),
        P("row", None, "col", None, None),
        P("row", None, "col", None, None),
        P("row", None, "col"),
        P(None, "row", None),
    )
    out_specs = P("row", None, None, "col", None)
    return jax.shard_map(shards, mesh=mesh, in_specs=in_specs, out_specs=out_specs, check_vma=False)
```
